256 devices in a mesh: prompt: 8 (over z_hi, y), group: 8 (over x, core), tensor: 4 (over z_lo).
Axes of the slice: x: 4, y: 4, z: 8 (z_hi: 2, z_lo: 4; z = z_hi * 4 + z_lo), core: 2. Of those that a mesh axis runs over, the one named last changes fastest.
Arguments:
- query: bfloat16 [64, 256, 5120], P(('prompt', 'group'), None, 'tensor'), may hold values from -33 to 33
- own_kv: bfloat16 [64, 256, 2, 1024], P(('prompt', 'group'), None, None, 'tensor'), may hold values from -6 to 6
- prompt_kv: bfloat16 [8, 2048, 2, 1024], P('group', ('prompt', 'tensor')), may hold values from -14 to 14
- d_out: bfloat16 [64, 256, 5120], P(('prompt', 'group'), None, 'tensor'), may hold values from -6 to 6
- prompt_of: int32 [8], replicated, may hold values from 0 to 7, as said below
- comp_len: int32 [64], P(('prompt', 'group')), may hold values from 1 to 256, 10240 in all
Outputs:
- attn_out: bfloat16 [64, 256, 5120], P(('prompt', 'group'), None, 'tensor')
- d_query: bfloat16 [64, 256, 5120], P(('prompt', 'group'), None, 'tensor')
- d_own_kv: bfloat16 [64, 256, 2, 1024], P(('prompt', 'group'), None, None, 'tensor')
- d_prompt_kv: bfloat16 [8, 2048, 2, 1024], P('group', ('prompt', 'tensor'))
The draws below stay inside these ranges and needn't reach their ends.
Inputs may be any that keep to these rules, and one draw needn't show every extreme that they name: `prompt_of`: a permutation: every prompt belongs to exactly one index of group. `comp_len`: some sample has all 256 tokens live.
All inputs are finite; a program needn't handle non-finite values. No bound on the sum of `comp_len` on one device may be relied on, other than what follows from the above.
Results may differ from the reference program's by a relative error of at most 0.035.
Values may be sent and summed in bfloat16 or wider, within the bound.
No kernel may reach another device: no remote copies, remote signals or barrier semaphores. Data moves between devices by JAX's collectives and lax.ppermute only.
A program may use at most 128 MiB of HBM per device.

```python
import math
import jax
import jax.numpy as jnp
import numpy as np
from jax import lax

HEADS = 40
KV_HEADS = 8
HEAD = 128
COMP = 256
PROMPTS = 8
SAMPLES = 64
PROMPT_LEN = 2048
N_GROUP = 8


def draw_prompt_of(key, part):
    key = jax.random.fold_in(key, 7)
    mixed_key = jax.random.fold_in(key, 4093)
    return jax.random.permutation(mixed_key, jnp.arange(PROMPTS, dtype=jnp.int32)).astype(jnp.int32)


def draw_prompt_kv(key, part):
    key = jax.random.fold_in(key, 1)
    first_key = jax.random.fold_in(key, 0)
    array_shape = (PROMPTS, PROMPT_LEN, 2, KV_HEADS * HEAD)
    values = jnp.clip(jax.random.normal(first_key, array_shape, jnp.float32), -6.0, 6.0)
    return values.astype(jnp.bfloat16)


def draw_query(key, part):
    key = jax.random.fold_in(key, 2)
    first_key = jax.random.fold_in(key, 0)
    array_shape = (SAMPLES, COMP, HEADS * HEAD)
    values = jnp.clip(jax.random.normal(first_key, array_shape, jnp.float32), -6.0, 6.0)
    return values.astype(jnp.bfloat16)


def block_levels(rng, dims, cuts, smallest, high):
    level, own = 1.0, jax.random.fold_in(rng, 6)
    for dim, blocks in cuts:
        steps = jnp.exp(jax.random.uniform(jax.random.fold_in(own, dim), (blocks,), jnp.float32, smallest / len(cuts), high / len(cuts)))
        level = level * jnp.repeat(steps, dims[dim] // blocks).reshape([-1 if axis == dim else 1 for axis in range(len(dims))])
    return level


def profile(amount, total, most, lean):
    portions = [(1 << 20) // math.isqrt(grade ** lean) + 1 for grade in range(2, amount + 1)]
    rest, holding = total - most - (amount - 1), [1] * (amount - 1)
    while rest > 0:
        movable = [i for i in range(amount - 1) if holding[i] < most]
        mass, remaining = sum([portions[i] for i in movable]), rest
        for i in movable:
            more = min(most - holding[i], max(1, remaining * portions[i] // mass), rest)
            holding[i] = holding[i] + more
            rest = rest - more
    return np.array([most] + holding)


def ragged_sizes(stream_key, number_of, total, most, slope):
    if number_of == 2:
        one = jax.random.randint(stream_key, (), max(1, total - most), min(most, total - 1) + 1)
        return jnp.stack([one, total - one])
    lengths = jnp.asarray(profile(number_of, total, most, slope), jnp.int32)
    pairs = (number_of - 1) // 2
    source_of, sink = lengths[1:1 + 2 * pairs:2], lengths[2:2 + 2 * pairs:2]
    room = jnp.minimum(source_of - 1, most - sink)
    passed = jax.random.randint(jax.random.fold_in(stream_key, 1), (pairs,), 0, 1 << 20) % (room + 1)
    lengths = lengths.at[1:1 + 2 * pairs:2].set(source_of - passed).at[2:2 + 2 * pairs:2].set(sink + passed)
    return lengths[jax.random.permutation(jax.random.fold_in(stream_key, 2), number_of)]


def noise(stream_key, shape, scale, reach, cuts=(), kind=jnp.bfloat16):
    drawn = jax.random.normal(stream_key, shape, jnp.float32) * scale
    if len(cuts) > 0:
        drawn = block_levels(stream_key, shape, cuts, -0.22, 0.18) * drawn
    return jnp.clip(drawn, min=-reach, max=reach).astype(kind)


def setup_inputs(seed: int = 0) -> dict:
    arg_keys = jax.random.split(jax.random.key(seed), 7)
    query = draw_query(jax.random.fold_in(arg_keys[6], 71), 0)
    own_kv = noise(arg_keys[1], (SAMPLES, COMP, 2, KV_HEADS * HEAD), 1.0, 6.0, ((0, 64), (3, 4)))
    prompt_kv = draw_prompt_kv(jax.random.fold_in(arg_keys[6], 71), 0)
    d_out = noise(arg_keys[3], (SAMPLES, COMP, HEADS * HEAD), 1.0, 6.0, ((0, 64), (2, 4)))
    prompt_of = draw_prompt_of(jax.random.fold_in(arg_keys[6], 71), 0)
    comp_len = ragged_sizes(arg_keys[5], SAMPLES, SAMPLES * COMP * 5 // 8, COMP, 0).astype(jnp.int32)
    return {"query": query, "own_kv": own_kv, "prompt_kv": prompt_kv, "d_out": d_out, "prompt_of": prompt_of, "comp_len": comp_len}


HIGH_PRECISION = lax.Precision.HIGHEST


def head_pass(head_queries, key_rows, value_rows, masked_grad, active):
    score_scale = HEAD ** -0.5
    query_float = head_queries.astype(jnp.float32)
    key_float = key_rows.astype(jnp.float32)
    value_float = value_rows.astype(jnp.float32)
    scores = jnp.einsum("rle,ke->rlk", query_float, key_float, precision=HIGH_PRECISION) * score_scale
    row_ids = jnp.arange(COMP, dtype=jnp.int32)[:, None]
    column_ids = jnp.arange(PROMPT_LEN + COMP, dtype=jnp.int32)[None, :]
    allowed = (column_ids < PROMPT_LEN) | (column_ids - PROMPT_LEN <= row_ids)
    scores = jnp.where(allowed[None], scores, -jnp.inf)
    highest = jnp.max(scores, axis=-1, keepdims=True)
    probs = jnp.exp(scores - highest)
    totals = jnp.sum(probs, axis=-1, keepdims=True)
    rounded_probs = probs.astype(jnp.bfloat16).astype(jnp.float32)
    output_float = jnp.einsum("rlk,ke->rle", rounded_probs, value_float, precision=HIGH_PRECISION) / totals
    attn_out = (output_float * active[None, :, None]).astype(jnp.bfloat16)
    grad_float = masked_grad.astype(jnp.float32)
    value_flow = jnp.einsum("rle,ke->rlk", grad_float, value_float, precision=HIGH_PRECISION)
    row_delta = jnp.sum(grad_float * attn_out.astype(jnp.float32), axis=-1, keepdims=True)
    shares = probs / totals
    rounded_shares = shares.astype(jnp.bfloat16).astype(jnp.float32)
    slopes = (shares * (value_flow - row_delta)).astype(jnp.bfloat16).astype(jnp.float32)
    d_query = (jnp.einsum("rlk,ke->rle", slopes, key_float, precision=HIGH_PRECISION) * score_scale).astype(jnp.bfloat16)
    key_grad = jnp.einsum("rlk,rle->ke", slopes, query_float, precision=HIGH_PRECISION) * score_scale
    value_grad = jnp.einsum("rlk,rle->ke", rounded_shares, grad_float, precision=HIGH_PRECISION)
    return attn_out, d_query, key_grad, value_grad


def reference(query, own_kv, prompt_kv, d_out, prompt_of, comp_len):
    head_ratio = HEADS // KV_HEADS
    total_rows = PROMPT_LEN + COMP

    def sample_step(prompt_grads, sample):
        which_prompt = prompt_of[sample % N_GROUP]
        prompt_rows = lax.dynamic_index_in_dim(prompt_kv, which_prompt, 0, keepdims=False)
        sample_rows = lax.dynamic_index_in_dim(own_kv, sample, 0, keepdims=False)
        sample_queries = lax.dynamic_index_in_dim(query, sample, 0, keepdims=False)
        sample_grad = lax.dynamic_index_in_dim(d_out, sample, 0, keepdims=False)
        length_now = lax.dynamic_index_in_dim(comp_len, sample, 0, keepdims=False)
        active = (jnp.arange(COMP, dtype=jnp.int32) < length_now).astype(jnp.float32)
        masked_grad = sample_grad * active[:, None].astype(jnp.bfloat16)
        grouped_queries = sample_queries.reshape(COMP, KV_HEADS, head_ratio, HEAD).transpose(1, 2, 0, 3)
        grouped_grad = masked_grad.reshape(COMP, KV_HEADS, head_ratio, HEAD).transpose(1, 2, 0, 3)
        all_rows = jnp.concatenate([prompt_rows, sample_rows], axis=0)
        all_rows = all_rows.reshape(total_rows, 2, KV_HEADS, HEAD).transpose(1, 2, 0, 3)
        attn_out, d_query, key_grad, value_grad = jax.vmap(head_pass, in_axes=(0, 0, 0, 0, None))(
            grouped_queries, all_rows[0], all_rows[1], grouped_grad, active)
        attn_out = attn_out.transpose(2, 0, 1, 3).reshape(COMP, HEADS * HEAD)
        d_query = d_query.transpose(2, 0, 1, 3).reshape(COMP, HEADS * HEAD)
        row_grads = jnp.stack([key_grad, value_grad], axis=0).transpose(2, 0, 1, 3)
        row_grads = row_grads.reshape(total_rows, 2, KV_HEADS * HEAD)
        prompt_grads = prompt_grads.at[which_prompt].add(row_grads[:PROMPT_LEN])
        return prompt_grads, (attn_out, d_query, row_grads[PROMPT_LEN:].astype(jnp.bfloat16))

    start_grads = jnp.zeros((PROMPTS, PROMPT_LEN, 2, KV_HEADS * HEAD), jnp.float32)
    prompt_grads, outputs = lax.scan(sample_step, start_grads, jnp.arange(SAMPLES, dtype=jnp.int32))
    attn_out, d_query, d_own_kv = outputs
    return attn_out, d_query, d_own_kv, prompt_grads.astype(jnp.bfloat16)
```

```python
import math
import jax
import jax.numpy as jnp
from jax import lax
from jax.experimental import pallas as pl
from jax.experimental.pallas import tpu as pltpu
from jax.sharding import Mesh, PartitionSpec as P

HEADS = 40
KV_HEADS = 8
HEAD = 128
RATIO = HEADS // KV_HEADS
ROWS = 256
SEG = 512
TILE = 256
SCALE = HEAD ** (-0.5)
LOG2 = SCALE * math.log2(math.e)
VMEM_LIMIT = 40 * 1024 * 1024

F32 = jnp.float32
BF16 = jnp.bfloat16


def dot_nt(a, b):
    return lax.dot_general(a, b, (((1,), (1,)), ((), ())), preferred_element_type=F32)


def dot_nn(a, b):
    return lax.dot_general(a, b, (((1,), (0,)), ((), ())), preferred_element_type=F32)


def tiles_of(refs):
    out, base = [], 0
    for ref in refs:
        rows = ref.shape[0]
        for start in range(0, rows, TILE):
            out.append((ref, start, base + start))
        base += rows
    return out


def fold(x, op):
    return op(x.reshape(TILE // 8, 8, x.shape[1]), axis=0)


def probs_kernel(len_ref, q_ref, g_ref, k0, k1, k2, k3, ko, p_ref, gs_ref, rt_ref, d0, d1, d2, d3, do, s_ref, acc_ref):
    r = pl.program_id(0) % RATIO
    q = q_ref[...]
    top = None
    for ref, start, row in tiles_of((k0, k1, k2, k3, ko)):
        s = dot_nt(ref[start : start + TILE, :], q)
        if ref is ko:
            key_ids = lax.broadcasted_iota(jnp.int32, s.shape, 0)
            row_ids = lax.broadcasted_iota(jnp.int32, s.shape, 1)
            s = jnp.where(key_ids <= row_ids, s, -jnp.inf)
        s_ref[row : row + TILE, :] = s
        part = fold(s, jnp.max)
        top = part if top is None else jnp.maximum(top, part)
    top = jnp.max(top, axis=0, keepdims=True) * LOG2
    total = jnp.zeros((8, ROWS), F32)
    for row in range(0, s_ref.shape[0], TILE):
        p = jnp.exp2(s_ref[row : row + TILE, :] * LOG2 - top)
        total = total + fold(p, jnp.sum)
        p_ref[0, row : row + TILE, :] = p.astype(BF16)
    rt = 1.0 / jnp.sum(total, axis=0, keepdims=True)
    rt_ref[0] = jnp.broadcast_to(rt, (8, ROWS))
    rows = lax.broadcasted_iota(jnp.int32, (ROWS, HEAD), 0)
    shrink = jnp.broadcast_to(rt, (HEAD, ROWS)).T
    gs = jnp.where(rows < len_ref[0], g_ref[...].astype(F32) * shrink, 0.0).astype(BF16)
    gs_ref[...] = gs

    @pl.when(r == 0)
    def _():
        acc_ref[...] = jnp.zeros_like(acc_ref)

    for row in range(0, s_ref.shape[0], TILE):
        acc_ref[row : row + TILE, :] += dot_nn(p_ref[0, row : row + TILE, :], gs)

    @pl.when(r == RATIO - 1)
    def _():
        for ref, start, row in tiles_of((d0, d1, d2, d3, do)):
            ref[start : start + TILE, :] = acc_ref[row : row + TILE, :].astype(BF16)


def slopes_kernel(q_ref, gs_ref, rt_ref, p_ref, v0, v1, v2, v3, vo, sl_ref, d0, d1, d2, d3, do, f_ref, acc_ref):
    r = pl.program_id(0) % RATIO
    q = q_ref[...]
    gs = gs_ref[...]
    delta = jnp.zeros((8, ROWS), F32)
    for ref, start, row in tiles_of((v0, v1, v2, v3, vo)):
        flow = dot_nt(ref[start : start + TILE, :], gs)
        f_ref[row : row + TILE, :] = flow
        delta = delta + fold(flow * p_ref[0, row : row + TILE, :].astype(F32), jnp.sum)
    delta = jnp.sum(delta, axis=0, keepdims=True) * rt_ref[0, 0:1, :]

    @pl.when(r == 0)
    def _():
        acc_ref[...] = jnp.zeros_like(acc_ref)

    for row in range(0, f_ref.shape[0], TILE):
        p = p_ref[0, row : row + TILE, :].astype(F32)
        sl = (p * (f_ref[row : row + TILE, :] - delta)).astype(BF16)
        sl_ref[0, row : row + TILE, :] = sl
        acc_ref[row : row + TILE, :] += dot_nn(sl, q)

    @pl.when(r == RATIO - 1)
    def _():
        for ref, start, row in tiles_of((d0, d1, d2, d3, do)):
            ref[start : start + TILE, :] = (acc_ref[row : row + TILE, :] * SCALE).astype(BF16)


def rows_kernel(len_ref, rt_ref, p_ref, sl_ref, k0, k1, k2, k3, ko, v0, v1, v2, v3, vo, o_ref, dq_ref, kt_ref, vt_ref):
    r = pl.program_id(0) % RATIO

    @pl.when(r == 0)
    def _():
        for ref, start, row in tiles_of((k0, k1, k2, k3, ko)):
            kt_ref[:, row : row + TILE] = ref[start : start + TILE, :].T
        for ref, start, row in tiles_of((v0, v1, v2, v3, vo)):
            vt_ref[:, row : row + TILE] = ref[start : start + TILE, :].T

    out = dot_nn(vt_ref[...], p_ref[0]) * rt_ref[0, 0:1, :]
    row_ids = lax.broadcasted_iota(jnp.int32, out.shape, 1)
    out = jnp.where(row_ids < len_ref[0], out, 0.0)
    o_ref[...] = out.T.astype(BF16)
    dq = dot_nn(kt_ref[...], sl_ref[0]) * SCALE
    dq_ref[...] = dq.T.astype(BF16)


def head_block(h, *_):
    return (0, h)


def group_block(h, *_):
    return (0, h // RATIO)


def plane(h, *_):
    return (h, 0, 0)


def attention_calls(keys):
    count = 2 * RATIO
    head_spec = pl.BlockSpec((ROWS, HEAD), head_block)
    seg_specs = [pl.BlockSpec((SEG, HEAD), group_block)] * 4 + [pl.BlockSpec((ROWS, HEAD), group_block)]
    plane_spec = pl.BlockSpec((1, keys, ROWS), plane)
    rt_spec = pl.BlockSpec((1, 8, ROWS), plane)
    params = pltpu.CompilerParams(dimension_semantics=("arbitrary",), vmem_limit_bytes=VMEM_LIMIT)
    head_shape = jax.ShapeDtypeStruct((ROWS, count * HEAD), BF16)
    seg_shapes = [jax.ShapeDtypeStruct((SEG, 2 * HEAD), BF16)] * 4 + [jax.ShapeDtypeStruct((ROWS, 2 * HEAD), BF16)]
    plane_shape = jax.ShapeDtypeStruct((count, keys, ROWS), BF16)
    rt_shape = jax.ShapeDtypeStruct((count, 8, ROWS), F32)
    scratch = [pltpu.VMEM((keys, ROWS), F32), pltpu.VMEM((keys, HEAD), F32)]
    work = 4 * count * keys * ROWS * HEAD
    cost = pl.CostEstimate(flops=2 * work, bytes_accessed=20 * 1024 * 1024, transcendentals=count * keys * ROWS)

    probs = pl.pallas_call(
        probs_kernel,
        grid_spec=pltpu.PrefetchScalarGridSpec(
            num_scalar_prefetch=1,
            grid=(count,),
            in_specs=[head_spec, head_spec] + seg_specs,
            out_specs=[plane_spec, head_spec, rt_spec] + seg_specs,
            scratch_shapes=scratch,
        ),
        out_shape=[plane_shape, head_shape, rt_shape] + seg_shapes,
        compiler_params=params,
        cost_estimate=cost,
        name="probs",
    )
    slopes = pl.pallas_call(
        slopes_kernel,
        grid=(count,),
        in_specs=[head_spec, head_spec, rt_spec, plane_spec] + seg_specs,
        out_specs=[plane_spec] + seg_specs,
        scratch_shapes=scratch,
        out_shape=[plane_shape] + seg_shapes,
        compiler_params=params,
        cost_estimate=cost,
        name="slopes",
    )
    rows = pl.pallas_call(
        rows_kernel,
        grid_spec=pltpu.PrefetchScalarGridSpec(
            num_scalar_prefetch=1,
            grid=(count,),
            in_specs=[rt_spec, plane_spec, plane_spec] + seg_specs + seg_specs,
            out_specs=[head_spec, head_spec],
            scratch_shapes=[pltpu.VMEM((HEAD, keys), BF16)] * 2,
        ),
        out_shape=[head_shape, head_shape],
        compiler_params=params,
        cost_estimate=cost,
        name="rows",
    )
    return probs, slopes, rows


def shift(x, axis, size, by):
    return lax.ppermute(x, axis, [(i, (i + by) % size) for i in range(size)])


def pick(blocks, which):
    low = jnp.where(which == 0, blocks[0], blocks[1])
    high = jnp.where(which == 2, blocks[2], blocks[3])
    return jnp.where(which < 2, low, high)


def group_move(block, source_of):
    chip = lax.axis_index("x")
    core = lax.axis_index("core")
    wanted = source_of[2 * chip + core]
    mate_wanted = source_of[2 * chip + 1 - core]
    blocks = [block] + [shift(block, "x", 4, by) for by in (1, 2, 3)]
    for_mate = pick(blocks, (chip - mate_wanted // 2) % 4)
    from_mate = shift(for_mate, "core", 2, 1)
    mine = pick(blocks, (chip - wanted // 2) % 4)
    return jnp.where(wanted % 2 == core, mine, from_mate)


def gather_rows(block, source_of):
    moved = group_move(block, source_of)
    parts = moved.reshape(64, 4, 256).transpose(1, 0, 2)
    parts = jnp.concatenate([parts, parts], axis=0)
    segment = lax.all_to_all(parts, ("z_hi", "z_lo"), 0, 0, tiled=True).reshape(SEG, 256)
    return [segment] + [shift(segment, "y", 4, by) for by in (1, 2, 3)]


def scatter_rows(segments, source_of):
    total = segments[0].astype(F32)
    for by in (1, 2, 3):
        total = total + shift(segments[by], "y", 4, -by).astype(F32)
    parts = total.astype(BF16).reshape(8, 64, 256)
    parts = lax.all_to_all(parts, ("z_hi", "z_lo"), 0, 0, tiled=True).astype(F32)
    block = (parts[:4] + parts[4:]).astype(BF16)
    block = block.transpose(1, 0, 2).reshape(64, 1024)
    return group_move(block, source_of)


def local(query, own_kv, prompt_kv, d_out, prompt_of, comp_len):
    queries, grads = query[0], d_out[0]
    own_keys, own_values = own_kv[0, :, 0], own_kv[0, :, 1]
    group_ids = lax.iota(jnp.int32, 8)
    owner_of = jnp.sum(jnp.where(prompt_of[None, :] == group_ids[:, None], group_ids[None, :], 0), axis=1)
    probs, slopes, rows = attention_calls(4 * SEG + ROWS)

    keys = gather_rows(prompt_kv[0, :, 0], prompt_of)
    values = gather_rows(prompt_kv[0, :, 1], prompt_of)
    p, scaled, rt, *value_grads = probs(comp_len, queries, grads, *keys, own_keys)
    value_block = scatter_rows(value_grads[:4], owner_of)
    sl, *key_grads = slopes(queries, scaled, rt, p, *values, own_values)
    key_block = scatter_rows(key_grads[:4], owner_of)
    out, d_query = rows(comp_len, rt, p, sl, *keys, own_keys, *values, own_values)

    d_own = jnp.stack([key_grads[4], value_grads[4]], axis=1)
    d_prompt = jnp.stack([key_block, value_block], axis=1)
    return out[None], d_query[None], d_own[None], d_prompt[None]


def solution(mesh):
    fine = Mesh(mesh.devices.reshape(2, 4, 4, 2, 4), ("z_hi", "y", "x", "core", "z_lo"))
    samples, group, rows = ("z_hi", "y", "x", "core"), ("x", "core"), ("z_hi", "y", "z_lo")
    in_specs = (
        P(samples, None, "z_lo"),
        P(samples, None, None, "z_lo"),
        P(group, rows, None, None),
        P(samples, None, "z_lo"),
        P(),
        P(samples),
    )
    out_specs = (
        P(samples, None, "z_lo"),
        P(samples, None, "z_lo"),
        P(samples, None, None, "z_lo"),
        P(group, rows, None, None),
    )
    return jax.shard_map(local, mesh=fine, in_specs=in_specs, out_specs=out_specs, check_vma=False)
```

```python
import math
import jax
import jax.numpy as jnp
from jax import lax
from jax.experimental import pallas as pl
from jax.experimental.pallas import tpu as pltpu
from jax.sharding import Mesh, PartitionSpec as P

HEADS = 40
KV_HEADS = 8
HEAD = 128
RATIO = HEADS // KV_HEADS
ROWS = 256
SEG = 512
TILE = 256
SCALE = HEAD ** (-0.5)
LOG2 = SCALE * math.log2(math.e)
VMEM_LIMIT = 60 * 1024 * 1024

F32 = jnp.float32
BF16 = jnp.bfloat16


def dot_nt(a, b):
    return lax.dot_general(a, b, (((1,), (1,)), ((), ())), preferred_element_type=F32)


def dot_nn(a, b):
    return lax.dot_general(a, b, (((1,), (0,)), ((), ())), preferred_element_type=F32)


def tiles_of(refs):
    out, base = [], 0
    for ref in refs:
        rows = ref.shape[0]
        for start in range(0, rows, TILE):
            out.append((ref, start, base + start))
        base += rows
    return out


def fold(x, op):
    return op(x.reshape(TILE // 8, 8, x.shape[1]), axis=0)


def store_segments(refs, acc_ref, scale):
    for ref, start, row in tiles_of(refs):
        part = acc_ref[:, row : row + TILE].T
        ref[start : start + TILE, :] = (part if scale is None else part * scale).astype(BF16)


def add_to(acc_ref, row, value, first):
    if first:
        acc_ref[:, row : row + TILE] = value
    else:
        acc_ref[:, row : row + TILE] += value


def probs_kernel(len_ref, q_ref, g_ref, k0, k1, k2, k3, ko, p_hbm, gs_ref, rt_ref, d0, d1, d2, d3, do, s_ref, p_ref, acc_ref, sems):
    base = pl.program_id(0) * RATIO
    tiles = tiles_of((k0, k1, k2, k3, ko))
    tops, totals, copies = {}, {}, []

    def score(r, ref, start, row):
        s = dot_nt(ref[start : start + TILE, :], q_ref[:, r * HEAD : (r + 1) * HEAD])
        if ref is ko:
            key_ids = lax.broadcasted_iota(jnp.int32, s.shape, 0)
            row_ids = lax.broadcasted_iota(jnp.int32, s.shape, 1)
            s = jnp.where(key_ids <= row_ids, s, -jnp.inf)
        s_ref[r % 2, row : row + TILE, :] = s
        part = fold(s, jnp.max)
        tops[r] = jnp.maximum(tops[r], part) if r in tops else part

    def weigh(r, top, row):
        p = jnp.exp2(s_ref[r % 2, row : row + TILE, :] * LOG2 - top)
        p_ref[r, row : row + TILE, :] = p.astype(BF16)
        part = fold(p, jnp.sum)
        totals[r] = totals[r] + part if r in totals else part

    def shrink(r):
        rt = 1.0 / jnp.sum(totals[r], axis=0, keepdims=True)
        rt_ref[r] = jnp.broadcast_to(rt, (8, ROWS))
        rows = lax.broadcasted_iota(jnp.int32, (ROWS, HEAD), 0)
        scaled = g_ref[:, r * HEAD : (r + 1) * HEAD].astype(F32) * jnp.broadcast_to(rt, (HEAD, ROWS)).T
        gs = jnp.where(rows < len_ref[0], scaled, 0.0).astype(BF16)
        gs_ref[:, r * HEAD : (r + 1) * HEAD] = gs
        return gs.T

    for step in range(RATIO + 2):
        now, last, older = step, step - 1, step - 2
        if 0 <= older < RATIO:
            gst = shrink(older)
        if 0 <= last < RATIO:
            top = jnp.max(tops[last], axis=0, keepdims=True) * LOG2
        for ref, start, row in tiles:
            if now < RATIO:
                score(now, ref, start, row)
            if 0 <= last < RATIO:
                weigh(last, top, row)
            if 0 <= older < RATIO:
                add_to(acc_ref, row, dot_nt(gst, p_ref[older, row : row + TILE, :]), older == 0)
        if 0 <= last < RATIO:
            copy = pltpu.make_async_copy(p_ref.at[last], p_hbm.at[base + last], sems.at[last])
            copy.start()
            copies.append(copy)
    store_segments((d0, d1, d2, d3, do), acc_ref, None)
    for copy in copies:
        copy.wait()


def slopes_kernel(q_ref, gs_ref, rt_ref, p_hbm, v0, v1, v2, v3, vo, sl_hbm, d0, d1, d2, d3, do, f_ref, p_ref, sl_ref, acc_ref, in_sems, out_sems):
    base = pl.program_id(0) * RATIO
    tiles = tiles_of((v0, v1, v2, v3, vo))
    deltas, copies, fetches = {}, [], []
    for r in range(RATIO):
        fetch = pltpu.make_async_copy(p_hbm.at[base + r], p_ref.at[r], in_sems.at[r])
        fetch.start()
        fetches.append(fetch)

    def flow(r, ref, start, row):
        f = dot_nt(ref[start : start + TILE, :], gs_ref[:, r * HEAD : (r + 1) * HEAD])
        f_ref[r % 2, row : row + TILE, :] = f
        part = fold(f * p_ref[r, row : row + TILE, :].astype(F32), jnp.sum)
        deltas[r] = deltas[r] + part if r in deltas else part

    for step in range(RATIO + 1):
        now, last = step, step - 1
        if now < RATIO:
            fetches[now].wait()
        if 0 <= last:
            delta = jnp.sum(deltas[last], axis=0, keepdims=True) * rt_ref[last, 0:1, :]
            qt = q_ref[:, last * HEAD : (last + 1) * HEAD].T
        for ref, start, row in tiles:
            if now < RATIO:
                flow(now, ref, start, row)
            if 0 <= last:
                p = p_ref[last, row : row + TILE, :].astype(F32)
                sl = (p * (f_ref[last % 2, row : row + TILE, :] - delta)).astype(BF16)
                sl_ref[last, row : row + TILE, :] = sl
                add_to(acc_ref, row, dot_nt(qt, sl), last == 0)
        if 0 <= last:
            copy = pltpu.make_async_copy(sl_ref.at[last], sl_hbm.at[base + last], out_sems.at[last])
            copy.start()
            copies.append(copy)
    store_segments((d0, d1, d2, d3, do), acc_ref, SCALE)
    for copy in copies:
        copy.wait()


def rows_kernel(len_ref, rt_ref, p_ref, sl_ref, k0, k1, k2, k3, ko, v0, v1, v2, v3, vo, o_ref, dq_ref, kt_ref, vt_ref):
    r = pl.program_id(0) % RATIO

    @pl.when(r == 0)
    def _():
        for ref, start, row in tiles_of((k0, k1, k2, k3, ko)):
            kt_ref[:, row : row + TILE] = ref[start : start + TILE, :].T
        for ref, start, row in tiles_of((v0, v1, v2, v3, vo)):
            vt_ref[:, row : row + TILE] = ref[start : start + TILE, :].T

    out = dot_nn(vt_ref[...], p_ref[0]) * rt_ref[0, 0:1, :]
    row_ids = lax.broadcasted_iota(jnp.int32, out.shape, 1)
    out = jnp.where(row_ids < len_ref[0], out, 0.0)
    o_ref[...] = out.T.astype(BF16)
    dq = dot_nn(kt_ref[...], sl_ref[0]) * SCALE
    dq_ref[...] = dq.T.astype(BF16)


def head_block(h, *_):
    return (0, h)


def group_block(h, *_):
    return (0, h // RATIO)


def plane(h, *_):
    return (h, 0, 0)


def attention_calls(keys):
    count = 2 * RATIO
    head_spec = pl.BlockSpec((ROWS, HEAD), head_block)
    seg_specs = [pl.BlockSpec((SEG, HEAD), group_block)] * 4 + [pl.BlockSpec((ROWS, HEAD), group_block)]
    plane_spec = pl.BlockSpec((1, keys, ROWS), plane)
    rt_spec = pl.BlockSpec((1, 8, ROWS), plane)
    params = pltpu.CompilerParams(dimension_semantics=("arbitrary",), vmem_limit_bytes=VMEM_LIMIT)
    head_shape = jax.ShapeDtypeStruct((ROWS, count * HEAD), BF16)
    seg_shapes = [jax.ShapeDtypeStruct((SEG, 2 * HEAD), BF16)] * 4 + [jax.ShapeDtypeStruct((ROWS, 2 * HEAD), BF16)]
    plane_shape = jax.ShapeDtypeStruct((count, keys, ROWS), BF16)
    rt_shape = jax.ShapeDtypeStruct((count, 8, ROWS), F32)
    work = 4 * count * keys * ROWS * HEAD
    cost = pl.CostEstimate(flops=2 * work, bytes_accessed=20 * 1024 * 1024, transcendentals=count * keys * ROWS)

    five_spec = pl.BlockSpec((ROWS, RATIO * HEAD), lambda l, *_: (0, l))
    wide_specs = [pl.BlockSpec((SEG, HEAD), lambda l, *_: (0, l))] * 4 + [pl.BlockSpec((ROWS, HEAD), lambda l, *_: (0, l))]
    five_rt = pl.BlockSpec((RATIO, 8, ROWS), lambda l, *_: (l, 0, 0))
    hbm = pl.BlockSpec(memory_space=pltpu.HBM)
    five_planes = pltpu.VMEM((RATIO, keys, ROWS), BF16)
    probs = pl.pallas_call(
        probs_kernel,
        grid_spec=pltpu.PrefetchScalarGridSpec(
            num_scalar_prefetch=1,
            grid=(2,),
            in_specs=[five_spec, five_spec] + wide_specs,
            out_specs=[hbm, five_spec, five_rt] + wide_specs,
            scratch_shapes=[
                pltpu.VMEM((2, keys, ROWS), F32),
                five_planes,
                pltpu.VMEM((HEAD, keys), F32),
                pltpu.SemaphoreType.DMA((RATIO,)),
            ],
        ),
        out_shape=[plane_shape, head_shape, rt_shape] + seg_shapes,
        compiler_params=params,
        cost_estimate=cost,
        name="probs",
    )
    slopes = pl.pallas_call(
        slopes_kernel,
        grid=(2,),
        in_specs=[five_spec, five_spec, five_rt, hbm] + wide_specs,
        out_specs=[hbm] + wide_specs,
        scratch_shapes=[
            pltpu.VMEM((2, keys, ROWS), F32),
            five_planes,
            five_planes,
            pltpu.VMEM((HEAD, keys), F32),
            pltpu.SemaphoreType.DMA((RATIO,)),
            pltpu.SemaphoreType.DMA((RATIO,)),
        ],
        out_shape=[plane_shape] + seg_shapes,
        compiler_params=params,
        cost_estimate=cost,
        name="slopes",
    )
    rows = pl.pallas_call(
        rows_kernel,
        grid_spec=pltpu.PrefetchScalarGridSpec(
            num_scalar_prefetch=1,
            grid=(count,),
            in_specs=[rt_spec, plane_spec, plane_spec] + seg_specs + seg_specs,
            out_specs=[head_spec, head_spec],
            scratch_shapes=[pltpu.VMEM((HEAD, keys), BF16)] * 2,
        ),
        out_shape=[head_shape, head_shape],
        compiler_params=params,
        cost_estimate=cost,
        name="rows",
    )
    return probs, slopes, rows


def shift(x, axis, size, by):
    return lax.ppermute(x, axis, [(i, (i + by) % size) for i in range(size)])


def pick(blocks, which):
    low = jnp.where(which == 0, blocks[0], blocks[1])
    high = jnp.where(which == 2, blocks[2], blocks[3])
    return jnp.where(which < 2, low, high)


def group_move(block, source_of, after=None):
    chip = lax.axis_index("x")
    core = lax.axis_index("core")
    wanted = source_of[2 * chip + core]
    mate_wanted = source_of[2 * chip + 1 - core]
    blocks = [block] + [shift(block, "x", 4, by) for by in (1, 2, 3)]
    for_mate = pick(blocks, (chip - mate_wanted // 2) % 4)
    if after is not None:
        for_mate, after = lax.optimization_barrier((for_mate, after))
    from_mate = shift(for_mate, "core", 2, 1)
    mine = pick(blocks, (chip - wanted // 2) % 4)
    return jnp.where(wanted % 2 == core, mine, from_mate), after


def z_exchange(parts):
    return lax.all_to_all(parts, ("z_hi", "z_lo"), 0, 0, tiled=True)


def z_gather(moved):
    parts = moved.reshape(64, 4, 256).transpose(1, 0, 2)
    return z_exchange(jnp.concatenate([parts, parts], axis=0)).reshape(SEG, 256)


def y_gather(segment):
    return [segment] + [shift(segment, "y", 4, by) for by in (1, 2, 3)]


def y_return(segments):
    return [segments[0]] + [shift(segments[by], "y", 4, -by) for by in (1, 2, 3)]


def z_return(segments):
    total = segments[0].astype(F32)
    for segment in segments[1:]:
        total = total + segment.astype(F32)
    parts = z_exchange(total.astype(BF16).reshape(8, 64, 256)).astype(F32)
    block = (parts[:4] + parts[4:]).astype(BF16)
    return block.transpose(1, 0, 2).reshape(64, 1024)


def local(query, own_kv, prompt_kv, d_out, prompt_of, comp_len):
    queries, grads = query[0], d_out[0]
    own_keys, own_values = own_kv[0, :, 0], own_kv[0, :, 1]
    group_ids = lax.iota(jnp.int32, 8)
    owner_of = jnp.sum(jnp.where(prompt_of[None, :] == group_ids[:, None], group_ids[None, :], 0), axis=1)
    probs, slopes, rows = attention_calls(4 * SEG + ROWS)

    key_block, value_block = prompt_kv[0, :, 0], prompt_kv[0, :, 1]
    key_block, value_block = group_move(key_block, prompt_of, value_block)
    key_segment = z_gather(key_block)
    value_block, _ = group_move(value_block, prompt_of)
    key_segment, value_block = lax.optimization_barrier((key_segment, value_block))
    keys = y_gather(key_segment)
    values = y_gather(z_gather(value_block))

    p, scaled, rt, *value_grads = probs(comp_len, queries, grads, *keys, own_keys)
    value_back = y_return(value_grads[:4])
    sl, *key_grads = slopes(queries, scaled, rt, p, *values, own_values)
    key_back = y_return(key_grads[:4])
    value_block, _ = group_move(z_return(value_back), owner_of)
    out, d_query = rows(comp_len, rt, p, sl, *keys, own_keys, *values, own_values)
    key_block, _ = group_move(z_return(key_back), owner_of)

    d_own = jnp.stack([key_grads[4], value_grads[4]], axis=1)
    d_prompt = jnp.stack([key_block, value_block], axis=1)
    return out[None], d_query[None], d_own[None], d_prompt[None]


def solution(mesh):
    fine = Mesh(mesh.devices.reshape(2, 4, 4, 2, 4), ("z_hi", "y", "x", "core", "z_lo"))
    samples, group, rows = ("z_hi", "y", "x", "core"), ("x", "core"), ("z_hi", "y", "z_lo")
    in_specs = (
        P(samples, None, "z_lo"),
        P(samples, None, None, "z_lo"),
        P(group, rows, None, None),
        P(samples, None, "z_lo"),
        P(),
        P(samples),
    )
    out_specs = (
        P(samples, None, "z_lo"),
        P(samples, None, "z_lo"),
        P(samples, None, None, "z_lo"),
        P(group, rows, None, None),
    )
    return jax.shard_map(local, mesh=fine, in_specs=in_specs, out_specs=out_specs, check_vma=False)
```

```python
import math
import jax
import jax.numpy as jnp
from jax import lax
from jax.experimental import pallas as pl
from jax.experimental.pallas import tpu as pltpu
from jax.sharding import Mesh, PartitionSpec as P

HEADS = 40
KV_HEADS = 8
HEAD = 128
RATIO = HEADS // KV_HEADS
ROWS = 256
SEG = 512
TILE = 256
SCALE = HEAD ** (-0.5)
LOG2 = SCALE * math.log2(math.e)
VMEM_LIMIT = 60 * 1024 * 1024

F32 = jnp.float32
BF16 = jnp.bfloat16


def dot_nt(a, b):
    return lax.dot_general(a, b, (((1,), (1,)), ((), ())), preferred_element_type=F32)


def dot_nn(a, b):
    return lax.dot_general(a, b, (((1,), (0,)), ((), ())), preferred_element_type=F32)


def tiles_of(refs):
    out, base = [], 0
    for ref in refs:
        rows = ref.shape[0]
        for start in range(0, rows, TILE):
            out.append((ref, start, base + start))
        base += rows
    return out


def fold(x, op):
    return op(x.reshape(TILE // 8, 8, x.shape[1]), axis=0)


def store_segments(refs, acc_ref, scale):
    for ref, start, row in tiles_of(refs):
        part = acc_ref[:, row : row + TILE].T
        ref[start : start + TILE, :] = (part if scale is None else part * scale).astype(BF16)


def add_to(acc_ref, row, value, first):
    if first:
        acc_ref[:, row : row + TILE] = value
    else:
        acc_ref[:, row : row + TILE] += value


def probs_kernel(len_ref, q_ref, g_ref, k0, k1, k2, k3, ko, p_hbm, gs_ref, rt_ref, d0, d1, d2, d3, do, s_ref, p_ref, acc_ref, sems):
    base = pl.program_id(0) * RATIO
    tiles = tiles_of((k0, k1, k2, k3, ko))
    tops, totals, copies = {}, {}, []

    def score(r, ref, start, row):
        s = dot_nt(ref[start : start + TILE, :], q_ref[:, r * HEAD : (r + 1) * HEAD])
        if ref is ko:
            key_ids = lax.broadcasted_iota(jnp.int32, s.shape, 0)
            row_ids = lax.broadcasted_iota(jnp.int32, s.shape, 1)
            s = jnp.where(key_ids <= row_ids, s, -jnp.inf)
        s_ref[r % 2, row : row + TILE, :] = s
        part = fold(s, jnp.max)
        tops[r] = jnp.maximum(tops[r], part) if r in tops else part

    def weigh(r, top, row):
        p = jnp.exp2(s_ref[r % 2, row : row + TILE, :] * LOG2 - top)
        p_ref[r, row : row + TILE, :] = p.astype(BF16)
        part = fold(p, jnp.sum)
        totals[r] = totals[r] + part if r in totals else part

    def shrink(r):
        rt = 1.0 / jnp.sum(totals[r], axis=0, keepdims=True)
        rt_ref[r] = jnp.broadcast_to(rt, (8, ROWS))
        rows = lax.broadcasted_iota(jnp.int32, (ROWS, HEAD), 0)
        scaled = g_ref[:, r * HEAD : (r + 1) * HEAD].astype(F32) * jnp.broadcast_to(rt, (HEAD, ROWS)).T
        gs = jnp.where(rows < len_ref[0], scaled, 0.0).astype(BF16)
        gs_ref[:, r * HEAD : (r + 1) * HEAD] = gs
        return gs.T

    for step in range(RATIO + 2):
        now, last, older = step, step - 1, step - 2
        if 0 <= older < RATIO:
            gst = shrink(older)
        if 0 <= last < RATIO:
            top = jnp.max(tops[last], axis=0, keepdims=True) * LOG2
        for ref, start, row in tiles:
            if now < RATIO:
                score(now, ref, start, row)
            if 0 <= last < RATIO:
                weigh(last, top, row)
            if 0 <= older < RATIO:
                add_to(acc_ref, row, dot_nt(gst, p_ref[older, row : row + TILE, :]), older == 0)
        if 0 <= last < RATIO:
            copy = pltpu.make_async_copy(p_ref.at[last], p_hbm.at[base + last], sems.at[last])
            copy.start()
            copies.append(copy)
    store_segments((d0, d1, d2, d3, do), acc_ref, None)
    for copy in copies:
        copy.wait()


def slopes_kernel(q_ref, gs_ref, rt_ref, p_hbm, k0, k1, k2, k3, ko, v0, v1, v2, v3, vo, dq_ref, d0, d1, d2, d3, do, f_ref, p_ref, sl_ref, acc_ref, kt_ref, sems):
    base = pl.program_id(0) * RATIO
    tiles = tiles_of((v0, v1, v2, v3, vo))
    deltas, fetches = {}, []
    for r in range(RATIO):
        fetch = pltpu.make_async_copy(p_hbm.at[base + r], p_ref.at[r], sems.at[r])
        fetch.start()
        fetches.append(fetch)
    for ref, start, row in tiles_of((k0, k1, k2, k3, ko)):
        kt_ref[:, row : row + TILE] = ref[start : start + TILE, :].T

    def flow(r, ref, start, row):
        f = dot_nt(ref[start : start + TILE, :], gs_ref[:, r * HEAD : (r + 1) * HEAD])
        f_ref[r % 2, row : row + TILE, :] = f
        part = fold(f * p_ref[r, row : row + TILE, :].astype(F32), jnp.sum)
        deltas[r] = deltas[r] + part if r in deltas else part

    for step in range(RATIO + 2):
        now, last, older = step, step - 1, step - 2
        if now < RATIO:
            fetches[now].wait()
        if 0 <= last < RATIO:
            delta = jnp.sum(deltas[last], axis=0, keepdims=True) * rt_ref[last, 0:1, :]
            qt = q_ref[:, last * HEAD : (last + 1) * HEAD].T
        if 0 <= older < RATIO:
            dq = dot_nn(kt_ref[...], sl_ref[older % 2]) * SCALE
            dq_ref[:, older * HEAD : (older + 1) * HEAD] = dq.T.astype(BF16)
        for ref, start, row in tiles:
            if now < RATIO:
                flow(now, ref, start, row)
            if 0 <= last < RATIO:
                p = p_ref[last, row : row + TILE, :].astype(F32)
                sl = (p * (f_ref[last % 2, row : row + TILE, :] - delta)).astype(BF16)
                sl_ref[last % 2, row : row + TILE, :] = sl
                add_to(acc_ref, row, dot_nt(qt, sl), last == 0)
    store_segments((d0, d1, d2, d3, do), acc_ref, SCALE)


def rows_kernel(base, len_ref, rt_ref, p_hbm, v0, v1, v2, v3, vo, *rest):
    o_ref, p_ref, vt_ref, sems = rest[-4:]
    fetches = []
    for r in range(RATIO):
        fetch = pltpu.make_async_copy(p_hbm.at[base + r], p_ref.at[r], sems.at[r])
        fetch.start()
        fetches.append(fetch)
    for ref, start, row in tiles_of((v0, v1, v2, v3, vo)):
        vt_ref[:, row : row + TILE] = ref[start : start + TILE, :].T
    for r in range(RATIO):
        fetches[r].wait()
        out = dot_nn(vt_ref[...], p_ref[r]) * rt_ref[r, 0:1, :]
        row_ids = lax.broadcasted_iota(jnp.int32, out.shape, 1)
        out = jnp.where(row_ids < len_ref[0], out, 0.0)
        o_ref[:, r * HEAD : (r + 1) * HEAD] = out.T.astype(BF16)


def attention_calls(keys):
    count = 2 * RATIO
    columns = lambda l, *_: (0, l)
    five_spec = pl.BlockSpec((ROWS, RATIO * HEAD), columns)
    own_spec = pl.BlockSpec((ROWS, HEAD), columns)
    seg_specs = [pl.BlockSpec((SEG, HEAD), columns)] * 4 + [own_spec]
    five_rt = pl.BlockSpec((RATIO, 8, ROWS), lambda l, *_: (l, 0, 0))
    hbm = pl.BlockSpec(memory_space=pltpu.HBM)
    five_planes = pltpu.VMEM((RATIO, keys, ROWS), BF16)
    score_planes = pltpu.VMEM((2, keys, ROWS), F32)
    sums = pltpu.VMEM((HEAD, keys), F32)
    sems = pltpu.SemaphoreType.DMA((RATIO,))
    params = pltpu.CompilerParams(dimension_semantics=("arbitrary",), vmem_limit_bytes=VMEM_LIMIT)
    head_shape = jax.ShapeDtypeStruct((ROWS, count * HEAD), BF16)
    own_shape = jax.ShapeDtypeStruct((ROWS, 2 * HEAD), BF16)
    seg_shapes = [jax.ShapeDtypeStruct((SEG, 2 * HEAD), BF16)] * 4 + [own_shape]
    plane_shape = jax.ShapeDtypeStruct((count, keys, ROWS), BF16)
    rt_shape = jax.ShapeDtypeStruct((count, 8, ROWS), F32)
    work = 4 * count * keys * ROWS * HEAD

    def cost(flops, exps):
        return pl.CostEstimate(flops=flops, bytes_accessed=20 * 1024 * 1024, transcendentals=exps)

    probs = pl.pallas_call(
        probs_kernel,
        grid_spec=pltpu.PrefetchScalarGridSpec(
            num_scalar_prefetch=1,
            grid=(2,),
            in_specs=[five_spec, five_spec] + seg_specs,
            out_specs=[hbm, five_spec, five_rt] + seg_specs,
            scratch_shapes=[score_planes, five_planes, sums, sems],
        ),
        out_shape=[plane_shape, head_shape, rt_shape] + seg_shapes,
        compiler_params=params,
        cost_estimate=cost(2 * work, count * keys * ROWS),
        name="probs",
    )
    slopes = pl.pallas_call(
        slopes_kernel,
        grid=(2,),
        in_specs=[five_spec, five_spec, five_rt, hbm] + seg_specs + seg_specs,
        out_specs=[five_spec] + seg_specs,
        scratch_shapes=[
            score_planes,
            five_planes,
            pltpu.VMEM((2, keys, ROWS), BF16),
            sums,
            pltpu.VMEM((HEAD, keys), BF16),
            sems,
        ],
        out_shape=[head_shape] + seg_shapes,
        compiler_params=params,
        cost_estimate=cost(2 * work, 0),
        name="slopes",
    )

    def rows(half, before, *operands):
        pinned = lambda spec: pl.BlockSpec(spec.block_shape, lambda i, *_: spec.index_map(half))
        return pl.pallas_call(
            lambda *refs: rows_kernel(half * RATIO, *refs),
            grid_spec=pltpu.PrefetchScalarGridSpec(
                num_scalar_prefetch=1,
                grid=(1,),
                in_specs=[pinned(five_rt), hbm]
                + [pinned(x) for x in seg_specs]
                + [pl.BlockSpec(memory_space=pl.ANY)] * len(before),
                out_specs=pinned(five_spec),
                scratch_shapes=[five_planes, pltpu.VMEM((HEAD, keys), BF16), sems],
            ),
            out_shape=head_shape,
            input_output_aliases={len(operands): 0} if before else {},
            compiler_params=params,
            cost_estimate=cost(work // 2, 0) if before else pl.CostEstimate(flops=1, bytes_accessed=1, transcendentals=0),
            name="rows",
        )(*operands, *before)

    return probs, slopes, rows


def shift(x, axis, size, by):
    return lax.ppermute(x, axis, [(i, (i + by) % size) for i in range(size)])


def route(chip, core, source_of):
    spot = 2 * chip + core
    wanted, mate_wanted = source_of[spot], source_of[spot ^ 1]

    def by_distance(source):
        distance = (chip + 4 - lax.shift_right_logical(source, 1)) & 3
        return distance == 0, distance == 2, distance < 2

    return by_distance(mate_wanted), by_distance(wanted), (wanted & 1) == core


def pick(blocks, selectors):
    first, third, low = selectors
    return jnp.where(low, jnp.where(first, blocks[0], blocks[1]), jnp.where(third, blocks[2], blocks[3]))


def x_spread(block):
    return [block] + [shift(block, "x", 4, by) for by in (1, 2, 3)]


def core_pick(blocks, routes, after=None):
    mate_route, own_route, same_core = routes
    for_mate = pick(blocks, mate_route)
    if after is not None:
        for_mate, after = lax.optimization_barrier((for_mate, after))
    from_mate = shift(for_mate, "core", 2, 1)
    return jnp.where(same_core, pick(blocks, own_route), from_mate), after


def z_exchange(parts):
    return lax.all_to_all(parts, ("z_hi", "z_lo"), 0, 0, tiled=True)


def z_gather(moved):
    parts = moved.reshape(64, 4, 256).transpose(1, 0, 2)
    return z_exchange(jnp.concatenate([parts, parts], axis=0)).reshape(SEG, 256)


def y_gather(segment):
    return [segment] + [shift(segment, "y", 4, by) for by in (1, 2, 3)]


def y_return(segments):
    return [segments[0]] + [shift(segments[by], "y", 4, -by) for by in (1, 2, 3)]


def sum_segments(segments):
    total = segments[0].astype(F32)
    for segment in segments[1:]:
        total = total + segment.astype(F32)
    return total.astype(BF16).reshape(8, 64, 256)


def z_sum(parts):
    parts = parts.astype(F32)
    block = (parts[:4] + parts[4:]).astype(BF16)
    return block.transpose(1, 0, 2).reshape(64, 1024)


def local(query, own_kv, prompt_kv, d_out, prompt_of, comp_len):
    queries, grads = query[0], d_out[0]
    own_keys, own_values = own_kv[0, :, 0], own_kv[0, :, 1]
    group_ids = lax.iota(jnp.int32, 8)
    owner_of = jnp.sum(jnp.where(prompt_of[None, :] == group_ids[:, None], group_ids[None, :], 0), axis=1)
    probs, slopes, rows = attention_calls(4 * SEG + ROWS)

    chip, core = lax.axis_index("x"), lax.axis_index("core")
    prompt_route, owner_route = route(chip, core, prompt_of), route(chip, core, owner_of)

    key_block, value_block = prompt_kv[0, :, 0], prompt_kv[0, :, 1]
    key_block, value_block = core_pick(x_spread(key_block), prompt_route, value_block)
    key_segment = z_gather(key_block)
    value_block, _ = core_pick(x_spread(value_block), prompt_route)
    key_segment, value_block = lax.optimization_barrier((key_segment, value_block))
    keys = y_gather(key_segment)
    value_segment = z_gather(value_block)
    values = y_gather(value_segment)
    queries, value_segment, owner_route = lax.optimization_barrier((queries, value_segment, owner_route))

    p, scaled, rt, *value_grads = probs(comp_len, queries, grads, *keys, own_keys)
    value_back = y_return(value_grads[:4])
    d_query, *key_grads = slopes(queries, scaled, rt, p, *keys, own_keys, *values, own_values)
    key_grads[4], *value_back = lax.optimization_barrier((key_grads[4], *value_back))
    key_back = y_return(key_grads[:4])
    operands = (comp_len, rt, p, *values, own_values)
    half = rows(0, (), *operands)
    value_parts = z_exchange(sum_segments(value_back))
    *key_back, half = lax.optimization_barrier((*key_back, half))
    key_sum, value_parts = lax.optimization_barrier((sum_segments(key_back), value_parts))
    key_parts = z_exchange(key_sum)
    value_blocks = x_spread(z_sum(value_parts))
    out = rows(1, (half,), *operands)
    key_parts, out, *value_blocks = lax.optimization_barrier((key_parts, out, *value_blocks))
    key_block, _ = core_pick(x_spread(z_sum(key_parts)), owner_route)
    value_block, _ = core_pick(value_blocks, owner_route)

    d_own = jnp.stack([key_grads[4], value_grads[4]], axis=1)
    d_prompt = jnp.stack([key_block, value_block], axis=1)
    return out[None], d_query[None], d_own[None], d_prompt[None]


def solution(mesh):
    fine = Mesh(mesh.devices.reshape(2, 4, 4, 2, 4), ("z_hi", "y", "x", "core", "z_lo"))
    samples, group, rows = ("z_hi", "y", "x", "core"), ("x", "core"), ("z_hi", "y", "z_lo")
    in_specs = (
        P(samples, None, "z_lo"),
        P(samples, None, None, "z_lo"),
        P(group, rows, None, None),
        P(samples, None, "z_lo"),
        P(),
        P(samples),
    )
    out_specs = (
        P(samples, None, "z_lo"),
        P(samples, None, "z_lo"),
        P(samples, None, None, "z_lo"),
        P(group, rows, None, None),
    )
    return jax.shard_map(local, mesh=fine, in_specs=in_specs, out_specs=out_specs, check_vma=False)
```

```python
import math
import jax
import jax.numpy as jnp
from jax import lax
from jax.experimental import pallas as pl
from jax.experimental.pallas import tpu as pltpu
from jax.sharding import Mesh, PartitionSpec as P

HEADS = 40
KV_HEADS = 8
HEAD = 128
RATIO = HEADS // KV_HEADS
ROWS = 256
SEG = 512
TILE = 256
SCALE = HEAD ** (-0.5)
LOG2 = SCALE * math.log2(math.e)
VMEM_LIMIT = 60 * 1024 * 1024

F32 = jnp.float32
BF16 = jnp.bfloat16


def dot_nt(a, b):
    return lax.dot_general(a, b, (((1,), (1,)), ((), ())), preferred_element_type=F32)


def dot_nn(a, b):
    return lax.dot_general(a, b, (((1,), (0,)), ((), ())), preferred_element_type=F32)


def tiles_of(refs):
    out, base = [], 0
    for ref in refs:
        rows = ref.shape[0]
        for start in range(0, rows, TILE):
            out.append((ref, start, base + start))
        base += rows
    return out


def fold(x, op):
    return op(x.reshape(TILE // 8, 8, x.shape[1]), axis=0)


def store_segments(refs, acc_ref, scale):
    for ref, start, row in tiles_of(refs):
        part = acc_ref[:, row : row + TILE].T
        ref[start : start + TILE, :] = (part if scale is None else part * scale).astype(BF16)


def add_to(acc_ref, row, value, first):
    if first:
        acc_ref[:, row : row + TILE] = value
    else:
        acc_ref[:, row : row + TILE] += value


def probs_kernel(len_ref, q_ref, g_ref, k0, k1, k2, k3, ko, p_hbm, gs_ref, rt_ref, d0, d1, d2, d3, do, s_ref, p_ref, acc_ref, sems):
    base = pl.program_id(0) * RATIO
    tiles = tiles_of((k0, k1, k2, k3, ko))
    tops, totals, copies = {}, {}, []

    def score(r, ref, start, row):
        s = dot_nt(ref[start : start + TILE, :], q_ref[:, r * HEAD : (r + 1) * HEAD])
        if ref is ko:
            key_ids = lax.broadcasted_iota(jnp.int32, s.shape, 0)
            row_ids = lax.broadcasted_iota(jnp.int32, s.shape, 1)
            s = jnp.where(key_ids <= row_ids, s, -jnp.inf)
        s_ref[r % 2, row : row + TILE, :] = s
        part = fold(s, jnp.max)
        tops[r] = jnp.maximum(tops[r], part) if r in tops else part

    def weigh(r, top, row):
        p = jnp.exp2(s_ref[r % 2, row : row + TILE, :] * LOG2 - top)
        p_ref[r, row : row + TILE, :] = p.astype(BF16)
        part = fold(p, jnp.sum)
        totals[r] = totals[r] + part if r in totals else part

    def shrink(r):
        rt = 1.0 / jnp.sum(totals[r], axis=0, keepdims=True)
        rt_ref[r] = jnp.broadcast_to(rt, (8, ROWS))
        rows = lax.broadcasted_iota(jnp.int32, (ROWS, HEAD), 0)
        scaled = g_ref[:, r * HEAD : (r + 1) * HEAD].astype(F32) * jnp.broadcast_to(rt, (HEAD, ROWS)).T
        gs = jnp.where(rows < len_ref[0], scaled, 0.0).astype(BF16)
        gs_ref[:, r * HEAD : (r + 1) * HEAD] = gs
        return gs.T

    for step in range(RATIO + 2):
        now, last, older = step, step - 1, step - 2
        if 0 <= older < RATIO:
            gst = shrink(older)
        if 0 <= last < RATIO:
            top = jnp.max(tops[last], axis=0, keepdims=True) * LOG2
        for ref, start, row in tiles:
            if now < RATIO:
                score(now, ref, start, row)
            if 0 <= last < RATIO:
                weigh(last, top, row)
            if 0 <= older < RATIO:
                add_to(acc_ref, row, dot_nt(gst, p_ref[older, row : row + TILE, :]), older == 0)
        if 0 <= last < RATIO:
            copy = pltpu.make_async_copy(p_ref.at[last], p_hbm.at[base + last], sems.at[last])
            copy.start()
            copies.append(copy)
    store_segments((d0, d1, d2, d3, do), acc_ref, None)
    for copy in copies:
        copy.wait()


def slopes_kernel(q_ref, gs_ref, rt_ref, p_hbm, k0, k1, k2, k3, ko, v0, v1, v2, v3, vo, dq_ref, d0, d1, d2, d3, do, f_ref, p_ref, sl_ref, acc_ref, kt_ref, sems):
    base = pl.program_id(0) * RATIO
    tiles = tiles_of((v0, v1, v2, v3, vo))
    deltas = {}

    def fetch(r):
        return pltpu.make_async_copy(p_hbm.at[r], p_ref.at[r], sems.at[r])

    @pl.when(base == 0)
    def _():
        for r in range(2 * RATIO):
            fetch(r).start()

    for ref, start, row in tiles_of((k0, k1, k2, k3, ko)):
        kt_ref[:, row : row + TILE] = ref[start : start + TILE, :].T

    def flow(r, ref, start, row):
        f = dot_nt(ref[start : start + TILE, :], gs_ref[:, r * HEAD : (r + 1) * HEAD])
        f_ref[r % 2, row : row + TILE, :] = f
        part = fold(f * p_ref[base + r, row : row + TILE, :].astype(F32), jnp.sum)
        deltas[r] = deltas[r] + part if r in deltas else part

    for step in range(RATIO + 2):
        now, last, older = step, step - 1, step - 2
        if now < RATIO:
            fetch(base + now).wait()
        if 0 <= last < RATIO:
            delta = jnp.sum(deltas[last], axis=0, keepdims=True) * rt_ref[last, 0:1, :]
            qt = q_ref[:, last * HEAD : (last + 1) * HEAD].T
        if 0 <= older < RATIO:
            dq = dot_nn(kt_ref[...], sl_ref[older % 2]) * SCALE
            dq_ref[:, older * HEAD : (older + 1) * HEAD] = dq.T.astype(BF16)
        for ref, start, row in tiles:
            if now < RATIO:
                flow(now, ref, start, row)
            if 0 <= last < RATIO:
                p = p_ref[base + last, row : row + TILE, :].astype(F32)
                sl = (p * (f_ref[last % 2, row : row + TILE, :] - delta)).astype(BF16)
                sl_ref[last % 2, row : row + TILE, :] = sl
                add_to(acc_ref, row, dot_nt(qt, sl), last == 0)
    store_segments((d0, d1, d2, d3, do), acc_ref, SCALE)


def rows_kernel(base, len_ref, rt_ref, p_hbm, v0, v1, v2, v3, vo, *rest):
    o_ref, p_ref, vt_ref, sems = rest[-4:]
    fetches = []
    for r in range(RATIO):
        fetch = pltpu.make_async_copy(p_hbm.at[base + r], p_ref.at[r], sems.at[r])
        fetch.start()
        fetches.append(fetch)
    for ref, start, row in tiles_of((v0, v1, v2, v3, vo)):
        vt_ref[:, row : row + TILE] = ref[start : start + TILE, :].T
    for r in range(RATIO):
        fetches[r].wait()
        out = dot_nn(vt_ref[...], p_ref[r]) * rt_ref[r, 0:1, :]
        row_ids = lax.broadcasted_iota(jnp.int32, out.shape, 1)
        out = jnp.where(row_ids < len_ref[0], out, 0.0)
        o_ref[:, r * HEAD : (r + 1) * HEAD] = out.T.astype(BF16)


def attention_calls(keys):
    count = 2 * RATIO
    columns = lambda l, *_: (0, l)
    five_spec = pl.BlockSpec((ROWS, RATIO * HEAD), columns)
    own_spec = pl.BlockSpec((ROWS, HEAD), columns)
    seg_specs = [pl.BlockSpec((SEG, HEAD), columns)] * 4 + [own_spec]
    five_rt = pl.BlockSpec((RATIO, 8, ROWS), lambda l, *_: (l, 0, 0))
    hbm = pl.BlockSpec(memory_space=pltpu.HBM)
    five_planes = pltpu.VMEM((RATIO, keys, ROWS), BF16)
    score_planes = pltpu.VMEM((2, keys, ROWS), F32)
    sums = pltpu.VMEM((HEAD, keys), F32)
    sems = pltpu.SemaphoreType.DMA((RATIO,))
    params = pltpu.CompilerParams(dimension_semantics=("arbitrary",), vmem_limit_bytes=VMEM_LIMIT)
    head_shape = jax.ShapeDtypeStruct((ROWS, count * HEAD), BF16)
    own_shape = jax.ShapeDtypeStruct((ROWS, 2 * HEAD), BF16)
    seg_shapes = [jax.ShapeDtypeStruct((SEG, 2 * HEAD), BF16)] * 4 + [own_shape]
    plane_shape = jax.ShapeDtypeStruct((count, keys, ROWS), BF16)
    rt_shape = jax.ShapeDtypeStruct((count, 8, ROWS), F32)
    work = 4 * count * keys * ROWS * HEAD

    def cost(flops, exps):
        return pl.CostEstimate(flops=flops, bytes_accessed=20 * 1024 * 1024, transcendentals=exps)

    probs = pl.pallas_call(
        probs_kernel,
        grid_spec=pltpu.PrefetchScalarGridSpec(
            num_scalar_prefetch=1,
            grid=(2,),
            in_specs=[five_spec, five_spec] + seg_specs,
            out_specs=[hbm, five_spec, five_rt] + seg_specs,
            scratch_shapes=[score_planes, five_planes, sums, sems],
        ),
        out_shape=[plane_shape, head_shape, rt_shape] + seg_shapes,
        compiler_params=params,
        cost_estimate=cost(2 * work, count * keys * ROWS),
        name="probs",
    )
    slopes = pl.pallas_call(
        slopes_kernel,
        grid=(2,),
        in_specs=[five_spec, five_spec, five_rt, hbm] + seg_specs + seg_specs,
        out_specs=[five_spec] + seg_specs,
        scratch_shapes=[
            score_planes,
            pltpu.VMEM((count, keys, ROWS), BF16),
            pltpu.VMEM((2, keys, ROWS), BF16),
            sums,
            pltpu.VMEM((HEAD, keys), BF16),
            pltpu.SemaphoreType.DMA((count,)),
        ],
        out_shape=[head_shape] + seg_shapes,
        compiler_params=params,
        cost_estimate=cost(2 * work, 0),
        name="slopes",
    )

    def rows(half, before, *operands):
        pinned = lambda spec: pl.BlockSpec(spec.block_shape, lambda i, *_: spec.index_map(half))
        return pl.pallas_call(
            lambda *refs: rows_kernel(half * RATIO, *refs),
            grid_spec=pltpu.PrefetchScalarGridSpec(
                num_scalar_prefetch=1,
                grid=(1,),
                in_specs=[pinned(five_rt), hbm]
                + [pinned(x) for x in seg_specs]
                + [pl.BlockSpec(memory_space=pl.ANY)] * len(before),
                out_specs=pinned(five_spec),
                scratch_shapes=[five_planes, pltpu.VMEM((HEAD, keys), BF16), sems],
            ),
            out_shape=head_shape,
            input_output_aliases={len(operands): 0} if before else {},
            compiler_params=params,
            cost_estimate=cost(work // 2, 0) if before else pl.CostEstimate(flops=1, bytes_accessed=1, transcendentals=0),
            name="rows",
        )(*operands, *before)

    return probs, slopes, rows


def shift(x, axis, size, by):
    return lax.ppermute(x, axis, [(i, (i + by) % size) for i in range(size)])


def route(chip, core, source_of):
    spot = 2 * chip + core
    wanted, mate_wanted = source_of[spot], source_of[spot ^ 1]

    def by_distance(source):
        distance = (chip + 4 - lax.shift_right_logical(source, 1)) & 3
        return distance == 0, distance == 2, distance < 2

    return by_distance(mate_wanted), by_distance(wanted), (wanted & 1) == core


def pick(blocks, selectors):
    first, third, low = selectors
    return jnp.where(low, jnp.where(first, blocks[0], blocks[1]), jnp.where(third, blocks[2], blocks[3]))


def x_spread(block):
    return [block] + [shift(block, "x", 4, by) for by in (1, 2, 3)]


def core_pick(blocks, routes, after=None):
    mate_route, own_route, same_core = routes
    for_mate = pick(blocks, mate_route)
    if after is not None:
        for_mate, after = lax.optimization_barrier((for_mate, after))
    from_mate = shift(for_mate, "core", 2, 1)
    return jnp.where(same_core, pick(blocks, own_route), from_mate), after


def z_exchange(parts):
    return lax.all_to_all(parts, ("z_hi", "z_lo"), 0, 0, tiled=True)


def z_gather(moved):
    parts = moved.reshape(64, 4, 256).transpose(1, 0, 2)
    return z_exchange(jnp.concatenate([parts, parts], axis=0)).reshape(SEG, 256)


def y_gather(segment):
    return [segment] + [shift(segment, "y", 4, by) for by in (1, 2, 3)]


def y_return(segments):
    return [segments[0]] + [shift(segments[by], "y", 4, -by) for by in (1, 2, 3)]


def sum_segments(segments):
    total = segments[0].astype(F32)
    for segment in segments[1:]:
        total = total + segment.astype(F32)
    return total.astype(BF16).reshape(8, 64, 256)


def z_sum(parts):
    parts = parts.astype(F32)
    block = (parts[:4] + parts[4:]).astype(BF16)
    return block.transpose(1, 0, 2).reshape(64, 1024)


def local(query, own_kv, prompt_kv, d_out, prompt_of, comp_len):
    queries, grads = query[0], d_out[0]
    own_keys, own_values = own_kv[0, :, 0], own_kv[0, :, 1]
    group_ids = lax.iota(jnp.int32, 8)
    owner_of = jnp.sum(jnp.where(prompt_of[None, :] == group_ids[:, None], group_ids[None, :], 0), axis=1)
    probs, slopes, rows = attention_calls(4 * SEG + ROWS)

    chip, core = lax.axis_index("x"), lax.axis_index("core")
    prompt_route, owner_route = route(chip, core, prompt_of), route(chip, core, owner_of)

    key_block, value_block = prompt_kv[0, :, 0], prompt_kv[0, :, 1]
    key_block, value_block = core_pick(x_spread(key_block), prompt_route, value_block)
    key_segment = z_gather(key_block)
    value_block, _ = core_pick(x_spread(value_block), prompt_route)
    key_segment, value_block, owner_route = lax.optimization_barrier((key_segment, value_block, owner_route))
    keys = y_gather(key_segment)
    value_segment = z_gather(value_block)
    values = y_gather(value_segment)
    queries, value_segment = lax.optimization_barrier((queries, value_segment))

    p, scaled, rt, *value_grads = probs(comp_len, queries, grads, *keys, own_keys)
    value_back = y_return(value_grads[:4])
    d_query, *key_grads = slopes(queries, scaled, rt, p, *keys, own_keys, *values, own_values)
    key_grads[4], *value_back = lax.optimization_barrier((key_grads[4], *value_back))
    key_back = y_return(key_grads[:4])
    operands = (comp_len, rt, p, *values, own_values)
    half = rows(0, (), *operands)
    value_parts = z_exchange(sum_segments(value_back))
    *key_back, half = lax.optimization_barrier((*key_back, half))
    key_sum, value_parts = lax.optimization_barrier((sum_segments(key_back), value_parts))
    key_parts = z_exchange(key_sum)
    value_blocks = x_spread(z_sum(value_parts))
    key_parts, *value_blocks = lax.optimization_barrier((key_parts, *value_blocks))
    key_blocks = x_spread(z_sum(key_parts))
    out = rows(1, (half,), *operands)
    out, *key_blocks = lax.optimization_barrier((out, *key_blocks))
    key_block, _ = core_pick(key_blocks, owner_route)
    value_block, _ = core_pick(value_blocks, owner_route)

    d_own = jnp.stack([key_grads[4], value_grads[4]], axis=1)
    d_prompt = jnp.stack([key_block, value_block], axis=1)
    return out[None], d_query[None], d_own[None], d_prompt[None]


def solution(mesh):
    fine = Mesh(mesh.devices.reshape(2, 4, 4, 2, 4), ("z_hi", "y", "x", "core", "z_lo"))
    samples, group, rows = ("z_hi", "y", "x", "core"), ("x", "core"), ("z_hi", "y", "z_lo")
    in_specs = (
        P(samples, None, "z_lo"),
        P(samples, None, None, "z_lo"),
        P(group, rows, None, None),
        P(samples, None, "z_lo"),
        P(),
        P(samples),
    )
    out_specs = (
        P(samples, None, "z_lo"),
        P(samples, None, "z_lo"),
        P(samples, None, None, "z_lo"),
        P(group, rows, None, None),
    )
    return jax.shard_map(local, mesh=fine, in_specs=in_specs, out_specs=out_specs, check_vma=False)
```

```python
import math
import jax
import jax.numpy as jnp
from jax import lax
from jax.experimental import pallas as pl
from jax.experimental.pallas import tpu as pltpu
from jax.sharding import Mesh, PartitionSpec as P

HEADS = 40
KV_HEADS = 8
HEAD = 128
RATIO = HEADS // KV_HEADS
ROWS = 256
SEG = 512
TILE = 256
SCALE = HEAD ** (-0.5)
LOG2 = SCALE * math.log2(math.e)
VMEM_LIMIT = 60 * 1024 * 1024

F32 = jnp.float32
BF16 = jnp.bfloat16


def dot_nt(a, b):
    return lax.dot_general(a, b, (((1,), (1,)), ((), ())), preferred_element_type=F32)


def dot_nn(a, b):
    return lax.dot_general(a, b, (((1,), (0,)), ((), ())), preferred_element_type=F32)


def tiles_of(refs):
    out, base = [], 0
    for ref in refs:
        rows = ref.shape[0]
        for start in range(0, rows, TILE):
            out.append((ref, start, base + start))
        base += rows
    return out


def fold(x, op):
    return op(x.reshape(TILE // 8, 8, x.shape[1]), axis=0)


def store_segments(refs, acc_ref, scale):
    for ref, start, row in tiles_of(refs):
        part = acc_ref[:, row : row + TILE].T
        ref[start : start + TILE, :] = (part if scale is None else part * scale).astype(BF16)


def add_to(acc_ref, row, value, first):
    if first:
        acc_ref[:, row : row + TILE] = value
    else:
        acc_ref[:, row : row + TILE] += value


def probs_kernel(len_ref, q_ref, g_ref, k0, k1, k2, k3, ko, p_hbm, gs_ref, rt_ref, d0, d1, d2, d3, do, s_ref, p_ref, acc_ref, sems):
    base = pl.program_id(0) * RATIO
    tiles = tiles_of((k0, k1, k2, k3, ko))
    tops, totals = {}, {}

    def store(r):
        return pltpu.make_async_copy(p_ref.at[r], p_hbm.at[r], sems.at[r])

    def score(r, ref, start, row):
        s = dot_nt(ref[start : start + TILE, :], q_ref[:, r * HEAD : (r + 1) * HEAD])
        if ref is ko:
            key_ids = lax.broadcasted_iota(jnp.int32, s.shape, 0)
            row_ids = lax.broadcasted_iota(jnp.int32, s.shape, 1)
            s = jnp.where(key_ids <= row_ids, s, -jnp.inf)
        s_ref[r % 2, row : row + TILE, :] = s
        part = fold(s, jnp.max)
        tops[r] = jnp.maximum(tops[r], part) if r in tops else part

    def weigh(r, top, row):
        p = jnp.exp2(s_ref[r % 2, row : row + TILE, :] * LOG2 - top)
        p_ref[base + r, row : row + TILE, :] = p.astype(BF16)
        part = fold(p, jnp.sum)
        totals[r] = totals[r] + part if r in totals else part

    def shrink(r):
        rt = 1.0 / jnp.sum(totals[r], axis=0, keepdims=True)
        rt_ref[r] = jnp.broadcast_to(rt, (8, ROWS))
        rows = lax.broadcasted_iota(jnp.int32, (ROWS, HEAD), 0)
        scaled = g_ref[:, r * HEAD : (r + 1) * HEAD].astype(F32) * jnp.broadcast_to(rt, (HEAD, ROWS)).T
        gs = jnp.where(rows < len_ref[0], scaled, 0.0).astype(BF16)
        gs_ref[:, r * HEAD : (r + 1) * HEAD] = gs
        return gs.T

    for step in range(RATIO + 2):
        now, last, older = step, step - 1, step - 2
        if 0 <= older < RATIO:
            gst = shrink(older)
        if 0 <= last < RATIO:
            top = jnp.max(tops[last], axis=0, keepdims=True) * LOG2
        for ref, start, row in tiles:
            if now < RATIO:
                score(now, ref, start, row)
            if 0 <= last < RATIO:
                weigh(last, top, row)
            if 0 <= older < RATIO:
                add_to(acc_ref, row, dot_nt(gst, p_ref[base + older, row : row + TILE, :]), older == 0)
        if 0 <= last < RATIO:
            store(base + last).start()
    store_segments((d0, d1, d2, d3, do), acc_ref, None)

    @pl.when(base > 0)
    def _():
        for r in range(2 * RATIO):
            store(r).wait()


def slopes_kernel(q_ref, gs_ref, rt_ref, p_hbm, k0, k1, k2, k3, ko, v0, v1, v2, v3, vo, dq_ref, d0, d1, d2, d3, do, f_ref, p_ref, sl_ref, acc_ref, kt_ref, sems):
    base = pl.program_id(0) * RATIO
    tiles = tiles_of((v0, v1, v2, v3, vo))
    deltas = {}

    def fetch(r):
        return pltpu.make_async_copy(p_hbm.at[r], p_ref.at[r], sems.at[r])

    @pl.when(base == 0)
    def _():
        for r in range(2 * RATIO):
            fetch(r).start()

    for ref, start, row in tiles_of((k0, k1, k2, k3, ko)):
        kt_ref[:, row : row + TILE] = ref[start : start + TILE, :].T

    def flow(r, ref, start, row):
        f = dot_nt(ref[start : start + TILE, :], gs_ref[:, r * HEAD : (r + 1) * HEAD])
        f_ref[r % 2, row : row + TILE, :] = f
        part = fold(f * p_ref[base + r, row : row + TILE, :].astype(F32), jnp.sum)
        deltas[r] = deltas[r] + part if r in deltas else part

    for step in range(RATIO + 2):
        now, last, older = step, step - 1, step - 2
        if now < RATIO:
            fetch(base + now).wait()
        if 0 <= last < RATIO:
            delta = jnp.sum(deltas[last], axis=0, keepdims=True) * rt_ref[last, 0:1, :]
            qt = q_ref[:, last * HEAD : (last + 1) * HEAD].T
        if 0 <= older < RATIO:
            dq = dot_nn(kt_ref[...], sl_ref[older % 2]) * SCALE
            dq_ref[:, older * HEAD : (older + 1) * HEAD] = dq.T.astype(BF16)
        for ref, start, row in tiles:
            if now < RATIO:
                flow(now, ref, start, row)
            if 0 <= last < RATIO:
                p = p_ref[base + last, row : row + TILE, :].astype(F32)
                sl = (p * (f_ref[last % 2, row : row + TILE, :] - delta)).astype(BF16)
                sl_ref[last % 2, row : row + TILE, :] = sl
                add_to(acc_ref, row, dot_nt(qt, sl), last == 0)
    store_segments((d0, d1, d2, d3, do), acc_ref, SCALE)


def rows_kernel(base, len_ref, rt_ref, p_hbm, v0, v1, v2, v3, vo, *rest):
    o_ref, p_ref, vt_ref, sems = rest[-4:]
    fetches = []
    for r in range(RATIO):
        fetch = pltpu.make_async_copy(p_hbm.at[base + r], p_ref.at[r], sems.at[r])
        fetch.start()
        fetches.append(fetch)
    for ref, start, row in tiles_of((v0, v1, v2, v3, vo)):
        vt_ref[:, row : row + TILE] = ref[start : start + TILE, :].T
    for r in range(RATIO):
        fetches[r].wait()
        out = dot_nn(vt_ref[...], p_ref[r]) * rt_ref[r, 0:1, :]
        row_ids = lax.broadcasted_iota(jnp.int32, out.shape, 1)
        out = jnp.where(row_ids < len_ref[0], out, 0.0)
        o_ref[:, r * HEAD : (r + 1) * HEAD] = out.T.astype(BF16)


def attention_calls(keys):
    count = 2 * RATIO
    columns = lambda l, *_: (0, l)
    five_spec = pl.BlockSpec((ROWS, RATIO * HEAD), columns)
    own_spec = pl.BlockSpec((ROWS, HEAD), columns)
    seg_specs = [pl.BlockSpec((SEG, HEAD), columns)] * 4 + [own_spec]
    five_rt = pl.BlockSpec((RATIO, 8, ROWS), lambda l, *_: (l, 0, 0))
    hbm = pl.BlockSpec(memory_space=pltpu.HBM)
    five_planes = pltpu.VMEM((RATIO, keys, ROWS), BF16)
    score_planes = pltpu.VMEM((2, keys, ROWS), F32)
    sums = pltpu.VMEM((HEAD, keys), F32)
    sems = pltpu.SemaphoreType.DMA((RATIO,))
    params = pltpu.CompilerParams(dimension_semantics=("arbitrary",), vmem_limit_bytes=VMEM_LIMIT)
    head_shape = jax.ShapeDtypeStruct((ROWS, count * HEAD), BF16)
    own_shape = jax.ShapeDtypeStruct((ROWS, 2 * HEAD), BF16)
    seg_shapes = [jax.ShapeDtypeStruct((SEG, 2 * HEAD), BF16)] * 4 + [own_shape]
    plane_shape = jax.ShapeDtypeStruct((count, keys, ROWS), BF16)
    rt_shape = jax.ShapeDtypeStruct((count, 8, ROWS), F32)
    work = 4 * count * keys * ROWS * HEAD

    def cost(flops, exps):
        return pl.CostEstimate(flops=flops, bytes_accessed=20 * 1024 * 1024, transcendentals=exps)

    probs = pl.pallas_call(
        probs_kernel,
        grid_spec=pltpu.PrefetchScalarGridSpec(
            num_scalar_prefetch=1,
            grid=(2,),
            in_specs=[five_spec, five_spec] + seg_specs,
            out_specs=[hbm, five_spec, five_rt] + seg_specs,
            scratch_shapes=[score_planes, pltpu.VMEM((count, keys, ROWS), BF16), sums, pltpu.SemaphoreType.DMA((count,))],
        ),
        out_shape=[plane_shape, head_shape, rt_shape] + seg_shapes,
        compiler_params=params,
        cost_estimate=cost(2 * work, count * keys * ROWS),
        name="probs",
    )
    slopes = pl.pallas_call(
        slopes_kernel,
        grid=(2,),
        in_specs=[five_spec, five_spec, five_rt, hbm] + seg_specs + seg_specs,
        out_specs=[five_spec] + seg_specs,
        scratch_shapes=[
            score_planes,
            pltpu.VMEM((count, keys, ROWS), BF16),
            pltpu.VMEM((2, keys, ROWS), BF16),
            sums,
            pltpu.VMEM((HEAD, keys), BF16),
            pltpu.SemaphoreType.DMA((count,)),
        ],
        out_shape=[head_shape] + seg_shapes,
        compiler_params=params,
        cost_estimate=cost(2 * work, 0),
        name="slopes",
    )

    def rows(half, before, *operands):
        pinned = lambda spec: pl.BlockSpec(spec.block_shape, lambda i, *_: spec.index_map(half))
        return pl.pallas_call(
            lambda *refs: rows_kernel(half * RATIO, *refs),
            grid_spec=pltpu.PrefetchScalarGridSpec(
                num_scalar_prefetch=1,
                grid=(1,),
                in_specs=[pinned(five_rt), hbm]
                + [pinned(x) for x in seg_specs]
                + [pl.BlockSpec(memory_space=pl.ANY)] * len(before),
                out_specs=pinned(five_spec),
                scratch_shapes=[five_planes, pltpu.VMEM((HEAD, keys), BF16), sems],
            ),
            out_shape=head_shape,
            input_output_aliases={len(operands): 0} if before else {},
            compiler_params=params,
            cost_estimate=cost(work // 2, 0) if before else pl.CostEstimate(flops=1, bytes_accessed=1, transcendentals=0),
            name="rows",
        )(*operands, *before)

    return probs, slopes, rows


def shift(x, axis, size, by):
    return lax.ppermute(x, axis, [(i, (i + by) % size) for i in range(size)])


def route(chip, core, source_of):
    spot = 2 * chip + core
    wanted, mate_wanted = source_of[spot], source_of[spot ^ 1]

    def by_distance(source):
        distance = (chip + 4 - lax.shift_right_logical(source, 1)) & 3
        return distance == 0, distance == 2, distance < 2

    return by_distance(mate_wanted), by_distance(wanted), (wanted & 1) == core


def pick(blocks, selectors):
    first, third, low = selectors
    return jnp.where(low, jnp.where(first, blocks[0], blocks[1]), jnp.where(third, blocks[2], blocks[3]))


def x_spread(block):
    return [block] + [shift(block, "x", 4, by) for by in (1, 2, 3)]


def core_pick(blocks, routes, after=None):
    mate_route, own_route, same_core = routes
    for_mate = pick(blocks, mate_route)
    if after is not None:
        for_mate, after = lax.optimization_barrier((for_mate, after))
    from_mate = shift(for_mate, "core", 2, 1)
    return jnp.where(same_core, pick(blocks, own_route), from_mate), after


def z_exchange(parts):
    return lax.all_to_all(parts, ("z_hi", "z_lo"), 0, 0, tiled=True)


def z_gather(moved):
    parts = moved.reshape(64, 4, 256).transpose(1, 0, 2)
    return z_exchange(jnp.concatenate([parts, parts], axis=0)).reshape(SEG, 256)


def y_gather(segment):
    return [segment] + [shift(segment, "y", 4, by) for by in (1, 2, 3)]


def y_return(segments):
    return [segments[0]] + [shift(segments[by], "y", 4, -by) for by in (1, 2, 3)]


def sum_segments(segments):
    total = segments[0].astype(F32)
    for segment in segments[1:]:
        total = total + segment.astype(F32)
    return total.astype(BF16).reshape(8, 64, 256)


def z_sum(parts):
    parts = parts.astype(F32)
    block = (parts[:4] + parts[4:]).astype(BF16)
    return block.transpose(1, 0, 2).reshape(64, 1024)


def local(query, own_kv, prompt_kv, d_out, prompt_of, comp_len):
    queries, grads = query[0], d_out[0]
    own_keys, own_values = own_kv[0, :, 0], own_kv[0, :, 1]
    group_ids = lax.iota(jnp.int32, 8)
    owner_of = jnp.sum(jnp.where(prompt_of[None, :] == group_ids[:, None], group_ids[None, :], 0), axis=1)
    probs, slopes, rows = attention_calls(4 * SEG + ROWS)

    chip, core = lax.axis_index("x"), lax.axis_index("core")
    prompt_route, owner_route = route(chip, core, prompt_of), route(chip, core, owner_of)

    key_block, value_block = prompt_kv[0, :, 0], prompt_kv[0, :, 1]
    key_block, value_block = core_pick(x_spread(key_block), prompt_route, value_block)
    key_segment = z_gather(key_block)
    value_block, _ = core_pick(x_spread(value_block), prompt_route)
    key_segment, value_block, owner_route = lax.optimization_barrier((key_segment, value_block, owner_route))
    keys = y_gather(key_segment)
    value_segment = z_gather(value_block)
    values = y_gather(value_segment)
    queries, value_segment = lax.optimization_barrier((queries, value_segment))

    p, scaled, rt, *value_grads = probs(comp_len, queries, grads, *keys, own_keys)
    value_back = y_return(value_grads[:4])
    d_query, *key_grads = slopes(queries, scaled, rt, p, *keys, own_keys, *values, own_values)
    key_grads[4], *value_back = lax.optimization_barrier((key_grads[4], *value_back))
    key_back = y_return(key_grads[:4])
    operands = (comp_len, rt, p, *values, own_values)
    half = rows(0, (), *operands)
    value_parts = z_exchange(sum_segments(value_back))
    *key_back, half = lax.optimization_barrier((*key_back, half))
    key_sum, value_parts = lax.optimization_barrier((sum_segments(key_back), value_parts))
    key_parts = z_exchange(key_sum)
    value_blocks = x_spread(z_sum(value_parts))
    key_parts, *value_blocks = lax.optimization_barrier((key_parts, *value_blocks))
    key_blocks = x_spread(z_sum(key_parts))
    out = rows(1, (half,), *operands)
    out, *key_blocks = lax.optimization_barrier((out, *key_blocks))
    key_block, _ = core_pick(key_blocks, owner_route)
    value_block, _ = core_pick(value_blocks, owner_route)

    d_own = jnp.stack([key_grads[4], value_grads[4]], axis=1)
    d_prompt = jnp.stack([key_block, value_block], axis=1)
    return out[None], d_query[None], d_own[None], d_prompt[None]


def solution(mesh):
    fine = Mesh(mesh.devices.reshape(2, 4, 4, 2, 4), ("z_hi", "y", "x", "core", "z_lo"))
    samples, group, rows = ("z_hi", "y", "x", "core"), ("x", "core"), ("z_hi", "y", "z_lo")
    in_specs = (
        P(samples, None, "z_lo"),
        P(samples, None, None, "z_lo"),
        P(group, rows, None, None),
        P(samples, None, "z_lo"),
        P(),
        P(samples),
    )
    out_specs = (
        P(samples, None, "z_lo"),
        P(samples, None, "z_lo"),
        P(samples, None, None, "z_lo"),
        P(group, rows, None, None),
    )
    return jax.shard_map(local, mesh=fine, in_specs=in_specs, out_specs=out_specs, check_vma=False)
```
